32 devices in a mesh: blk: 4 (over y, x), grp: 8 (over z, core).
Axes of the slice: x: 2, y: 2, z: 4, core: 2. Of those that a mesh axis runs over, the one named last changes fastest.
Arguments:
- image_embeds: bfloat16 [512, 1152], P(('blk', 'grp')), may hold values from -6 to 6
- text_embeds: bfloat16 [512, 1152], P(('blk', 'grp')), may hold values from -6 to 6
Outputs:
- image_grads: float32 [512, 1152], P(('blk', 'grp'))
- text_grads: float32 [512, 1152], P(('blk', 'grp'))
The draws below stay inside these ranges and needn't reach their ends.
All inputs are finite; a program needn't handle non-finite values.
Results may differ from the reference program's by a relative error of at most 0.011.
Values may be sent and summed in bfloat16 or wider, within the bound.
A program may use at most 64 MiB of HBM per device.

```python
import jax
import jax.numpy as jnp
from jax import lax

D = 1152
ROWS = 16
BATCH = 512
N_BLK = 4
N_GRP = 8


def levels(stream_key, dims, shards, least, top_value):
    gain, own = 1.0, jax.random.fold_in(stream_key, 6)
    for axis_at, parts in shards:
        steps = jnp.exp(jax.random.uniform(jax.random.fold_in(own, axis_at), (parts,), jnp.float32, least / len(shards), top_value / len(shards)))
        gain = gain * jnp.repeat(steps, dims[axis_at] // parts).reshape([-1 if axis == axis_at else 1 for axis in range(len(dims))])
    return gain


def normal_values(rng, dims, width, bound, pieces=(), kind=jnp.bfloat16):
    entries = width * jax.random.normal(rng, dims, jnp.float32)
    if pieces:
        entries = entries * levels(rng, dims, pieces, -0.22, 0.18)
    return jnp.clip(entries, -bound, bound).astype(kind)


def setup_inputs(seed: int = 0) -> dict:
    streams_of = jax.random.split(jax.random.key(seed), 3)
    return {
        "image_embeds": normal_values(streams_of[0], (BATCH, D), 1.0, 6.0, ((0, 32),)),
        "text_embeds": normal_values(streams_of[1], (BATCH, D), 1.0, 6.0, ((0, 32),)),
    }


LOGIT_SCALE = 0.044
LOGIT_BIAS = -4.0


def reference(image_embeds, text_embeds):
    batch_size, feat_width = image_embeds.shape
    group_rows = ROWS * N_GRP
    text_split = text_embeds.reshape(N_BLK, N_GRP, ROWS, feat_width).astype(jnp.float32)
    text_ids = jnp.arange(batch_size, dtype=jnp.int32)

    def visit(text_total, block_index):
        begin_row = (block_index * group_rows).astype(jnp.int32)
        image_block = lax.dynamic_slice_in_dim(image_embeds, begin_row, group_rows, 0)
        logits = LOGIT_SCALE * lax.dot_general(image_block, text_embeds, (((1,), (1,)), ((), ())), preferred_element_type=jnp.float32) + LOGIT_BIAS
        image_ids = begin_row + jnp.arange(group_rows, dtype=jnp.int32)
        labels = (image_ids[:, None] == text_ids[None, :]).astype(jnp.float32)
        weights = (jax.nn.sigmoid(logits) - labels).astype(jnp.bfloat16)
        weight_split = weights.reshape(group_rows, N_BLK, N_GRP, ROWS).astype(jnp.float32)
        partials = LOGIT_SCALE * jnp.einsum("iogr,ogrd->gid", weight_split, text_split, precision=lax.Precision.HIGHEST)
        partials = lax.optimization_barrier(partials.astype(jnp.bfloat16)).astype(jnp.float32)
        image_part = jnp.sum(partials, axis=0)
        text_total = text_total + LOGIT_SCALE * lax.dot_general(weights, image_block, (((0,), (0,)), ((), ())), preferred_element_type=jnp.float32)
        return text_total, image_part

    text_grads, image_parts = lax.scan(visit, jnp.zeros((batch_size, feat_width), jnp.float32), jnp.arange(N_BLK, dtype=jnp.int32))
    return image_parts.reshape(batch_size, feat_width), text_grads
```

```python
import functools

import jax
import jax.numpy as jnp
from jax import lax
from jax.experimental import pallas as pl
from jax.experimental.pallas import tpu as pltpu
from jax.sharding import PartitionSpec as P

LOGIT_SCALE = 0.044
LOGIT_BIAS = -4.0
MESH = pl.DeviceIdType.MESH


def offsets(count, inner):
    return [(o, i) for o in range(count // inner) for i in range(inner)]


def moved(index, count, inner, step, sign):
    outer = lax.rem(index // inner + sign * step[0] + count // inner, count // inner)
    return outer * inner + lax.rem(index % inner + sign * step[1] + inner, inner)


def kernel(
    n_blk, n_grp, blk_inner, pair, rows, chunk,
    image_ref, text_ref, image_out, text_out,
    images, texts, image_send, text_send, image_got, text_got, text_sum, image_own,
    local_sem, gi_send, gi_recv, gt_send, gt_recv, si_send, si_recv, st_send, st_recv,
):
    blk, grp = lax.axis_index("blk"), lax.axis_index("grp")
    image_steps = [(b, c) for b in offsets(n_blk, blk_inner) for c in range(pair)]
    text_steps = list(range(n_grp // pair))

    def image_peer(step, sign):
        return (moved(blk, n_blk, blk_inner, step[0], sign), moved(grp, n_grp, pair, (0, step[1]), sign))

    def text_peer(step, sign):
        return (blk, moved(grp, n_grp, pair, (step, 0), sign))

    image_slots = range(1, len(image_steps))
    text_slots = range(1, len(text_steps))

    own_image = pltpu.make_async_copy(image_ref, images.at[pl.ds(0, rows)], local_sem.at[0])
    own_text = pltpu.make_async_copy(text_ref, texts.at[pl.ds(0, rows)], local_sem.at[1])
    own_text.start()
    own_image.start()

    barrier = pltpu.get_barrier_semaphore()
    for s in image_slots:
        pl.semaphore_signal(barrier, inc=1, device_id=image_peer(image_steps[s], 1), device_id_type=MESH)
    for s in text_slots:
        pl.semaphore_signal(barrier, inc=1, device_id=text_peer(text_steps[s], 1), device_id_type=MESH)
    own_text.wait()
    own_image.wait()
    pl.semaphore_wait(barrier, len(image_slots) + len(text_slots))

    def remote(src, dst, send, recv, slot, device):
        return pltpu.make_async_remote_copy(
            src_ref=src, dst_ref=dst, send_sem=send.at[slot], recv_sem=recv.at[slot],
            device_id=device, device_id_type=MESH,
        )

    def part(ref, slot):
        return ref.at[pl.ds(slot * rows, rows)]

    text_gather = [
        remote(part(texts, 0), part(texts, s), gt_send, gt_recv, s, text_peer(text_steps[s], 1))
        for s in text_slots
    ]
    image_gather = [
        remote(part(images, 0), part(images, s), gi_send, gi_recv, s, image_peer(image_steps[s], 1))
        for s in image_slots
    ]
    for copy in text_gather + image_gather:
        copy.start()
    for copy in text_gather + image_gather:
        copy.wait_recv()

    total = images.shape[0]

    def weights_of(begin, is_first):
        logits = LOGIT_SCALE * lax.dot_general(
            images[pl.ds(begin, chunk)], texts[...], (((1,), (1,)), ((), ())),
            preferred_element_type=jnp.float32,
        ) + LOGIT_BIAS
        row = lax.broadcasted_iota(jnp.int32, logits.shape, 0) + begin
        column = lax.broadcasted_iota(jnp.int32, logits.shape, 1)
        labels = jnp.where((row == column) & (row < rows), 1.0, 0.0)
        return (lax.logistic(logits) - labels).astype(jnp.bfloat16)

    def image_terms(weights):
        return LOGIT_SCALE * jnp.dot(weights, texts[...], preferred_element_type=jnp.float32)

    def text_terms(weights, begin):
        return LOGIT_SCALE * lax.dot_general(
            weights, images[pl.ds(begin, chunk)], (((0,), (0,)), ((), ())),
            preferred_element_type=jnp.float32,
        )

    image_scatter = [
        remote(part(image_send, s), image_got.at[s], si_send, si_recv, s, image_peer(image_steps[s], -1))
        for s in image_slots
    ]
    text_scatter = [
        remote(part(text_send, s), text_got.at[s], st_send, st_recv, s, text_peer(text_steps[s], -1))
        for s in text_slots
    ]

    weights = weights_of(0, True)
    terms = image_terms(weights)
    image_own[...] = terms[:rows]
    image_send[pl.ds(0, chunk)] = terms.astype(jnp.bfloat16)
    if total == chunk:
        for copy in image_scatter:
            copy.start()
        text_sum[...] = text_terms(weights, 0)
    else:
        text_sum[...] = text_terms(weights, 0)

        def later(at, carry):
            begin = pl.multiple_of(at * chunk, chunk)
            weights = weights_of(begin, False)
            image_send[pl.ds(begin, chunk)] = image_terms(weights).astype(jnp.bfloat16)
            text_sum[...] += text_terms(weights, begin)
            return carry

        lax.fori_loop(1, total // chunk, later, 0)
        for copy in image_scatter:
            copy.start()
    text_send[...] = text_sum[...].astype(jnp.bfloat16)
    for copy in text_scatter:
        copy.start()

    for copy in image_scatter:
        copy.wait_recv()
    grads = image_own[...]
    for s in image_slots:
        grads += image_got[s].astype(jnp.float32)
    image_out[...] = grads
    for copy in text_scatter:
        copy.wait_recv()
    grads = text_sum[pl.ds(0, rows)]
    for s in text_slots:
        grads += text_got[s].astype(jnp.float32)
    text_out[...] = grads
    for copy in text_gather + image_gather + image_scatter + text_scatter:
        copy.wait_send()


def local(n_blk, n_grp, image_embeds, text_embeds):
    rows, width = image_embeds.shape
    pair = 2 if n_grp % 2 == 0 else 1
    blk_inner = 2 if n_blk % 2 == 0 else 1
    n_image, n_text = n_blk * pair, n_grp // pair
    total = n_image * rows
    chunk = 128 if total % 128 == 0 else total
    bf16, f32 = jnp.bfloat16, jnp.float32
    out = jax.ShapeDtypeStruct((rows, width), f32)
    return pl.pallas_call(
        functools.partial(kernel, n_blk, n_grp, blk_inner, pair, rows, chunk),
        out_shape=(out, out),
        in_specs=[pl.BlockSpec(memory_space=pl.ANY)] * 2,
        out_specs=[pl.BlockSpec(memory_space=pltpu.VMEM)] * 2,
        scratch_shapes=[
            pltpu.VMEM((total, width), bf16),
            pltpu.VMEM((n_text * rows, width), bf16),
            pltpu.VMEM((total, width), bf16),
            pltpu.VMEM((n_text * rows, width), bf16),
            pltpu.VMEM((n_image, rows, width), bf16),
            pltpu.VMEM((n_text, rows, width), bf16),
            pltpu.VMEM((n_text * rows, width), f32),
            pltpu.VMEM((rows, width), f32),
            pltpu.SemaphoreType.DMA((2,)),
            *[pltpu.SemaphoreType.DMA((n,)) for n in (n_image, n_image, n_text, n_text) * 2],
        ],
        compiler_params=pltpu.CompilerParams(
            collective_id=0, has_side_effects=True, vmem_limit_bytes=40 * 1024 * 1024
        ),
    )(image_embeds, text_embeds)


def solution(mesh):
    placed = (P(("blk", "grp"), None), P(("blk", "grp"), None))
    return jax.shard_map(
        functools.partial(local, mesh.shape["blk"], mesh.shape["grp"]),
        mesh=mesh,
        in_specs=placed,
        out_specs=placed,
        check_vma=False,
    )
```

```python
import functools

import jax
import jax.numpy as jnp
from jax import lax
from jax.experimental import pallas as pl
from jax.experimental.pallas import tpu as pltpu
from jax.sharding import PartitionSpec as P

LOGIT_SCALE = 0.044
LOGIT_BIAS = -4.0
SPLIT = 1
TEXT_FIRST = True
MESH = pl.DeviceIdType.MESH


def offsets(count, inner):
    return [(o, i) for o in range(count // inner) for i in range(inner)]


def moved(index, count, inner, step, sign):
    outer = lax.rem(index // inner + sign * step[0] + count // inner, count // inner)
    return outer * inner + lax.rem(index % inner + sign * step[1] + inner, inner)


def kernel(
    n_blk, n_grp, blk_inner, pair, rows, chunk,
    image_ref, text_ref, outs,
    images, texts, image_send, text_send, image_got, text_got, text_sum, image_own,
    local_sem, gi_send, gi_recv, gt_send, gt_recv, si_send, si_recv, st_send, st_recv,
):
    blk, grp = lax.axis_index("blk"), lax.axis_index("grp")
    image_steps = [(b, c) for b in offsets(n_blk, blk_inner) for c in range(pair)]
    text_steps = list(range(n_grp // pair))

    def image_peer(step, sign):
        return (moved(blk, n_blk, blk_inner, step[0], sign), moved(grp, n_grp, pair, (0, step[1]), sign))

    def text_peer(step, sign):
        return (blk, moved(grp, n_grp, pair, (step, 0), sign))

    image_slots = range(1, len(image_steps))
    text_slots = range(1, len(text_steps))

    own_image = pltpu.make_async_copy(image_ref, images.at[pl.ds(0, rows)], local_sem.at[0])
    own_text = pltpu.make_async_copy(text_ref, texts.at[pl.ds(0, rows)], local_sem.at[1])

    barrier = pltpu.get_barrier_semaphore()
    for s in image_slots:
        pl.semaphore_signal(barrier, inc=1, device_id=image_peer(image_steps[s], 1), device_id_type=MESH)
    for s in text_slots:
        pl.semaphore_signal(barrier, inc=1, device_id=text_peer(text_steps[s], 1), device_id_type=MESH)
    pl.semaphore_wait(barrier, len(image_slots) + len(text_slots))

    def remote(src, dst, send, recv, slot, device):
        return pltpu.make_async_remote_copy(
            src_ref=src, dst_ref=dst, send_sem=send.at[slot], recv_sem=recv.at[slot],
            device_id=device, device_id_type=MESH,
        )

    def part(ref, slot):
        return ref.at[pl.ds(slot * rows, rows)]

    text_gather = [
        remote(text_ref, part(texts, s), gt_send, gt_recv, s, text_peer(text_steps[s], 1))
        for s in text_slots
    ]
    image_gather = [
        remote(image_ref, part(images, s), gi_send, gi_recv, s, image_peer(image_steps[s], 1))
        for s in image_slots
    ]
    for copy in text_gather + image_gather:
        copy.start()
    own_text.start()
    own_image.start()
    total = images.shape[0]

    def weights_of(begin):
        logits = LOGIT_SCALE * lax.dot_general(
            images[pl.ds(begin, chunk)], texts[...], (((1,), (1,)), ((), ())),
            preferred_element_type=jnp.float32,
        ) + LOGIT_BIAS
        row = lax.broadcasted_iota(jnp.int32, logits.shape, 0) + begin
        column = lax.broadcasted_iota(jnp.int32, logits.shape, 1)
        labels = jnp.where((row == column) & (row < rows), 1.0, 0.0)
        return (lax.logistic(logits) - labels).astype(jnp.bfloat16)

    def image_terms(weights):
        return LOGIT_SCALE * jnp.dot(weights, texts[...], preferred_element_type=jnp.float32)

    def text_terms(weights, begin, count):
        return LOGIT_SCALE * lax.dot_general(
            weights, images[pl.ds(begin, count)], (((0,), (0,)), ((), ())),
            preferred_element_type=jnp.float32,
        )

    image_scatter = [
        remote(part(image_send, s), image_got.at[s], si_send, si_recv, s, image_peer(image_steps[s], -1))
        for s in image_slots
    ]
    text_scatter = [
        remote(part(text_send, s), text_got.at[s], st_send, st_recv, s, text_peer(text_steps[s], -1))
        for s in text_slots
    ]

    def arrived(begin):
        for copy in image_gather[max(begin // rows - 1, 0):(begin + chunk) // rows - 1]:
            copy.wait_recv()

    own_text.wait()
    own_image.wait()
    for copy in text_gather:
        copy.wait_recv()
    if total <= 256:
        parts = []
        for begin in range(0, total, chunk):
            arrived(begin)
            parts.append(weights_of(begin))
            if TEXT_FIRST and begin + chunk == total:
                text_sum[...] = text_terms(jnp.concatenate(parts), 0, total)
                text_send[...] = text_sum[...].astype(jnp.bfloat16)
                for copy in text_scatter:
                    copy.start()
            terms = image_terms(parts[-1])
            if begin == 0:
                image_own[...] = terms[:rows]
            image_send[pl.ds(begin, chunk)] = terms.astype(jnp.bfloat16)
            for copy in image_scatter[max(begin // rows - 1, 0):(begin + chunk) // rows - 1]:
                copy.start()
        if not TEXT_FIRST:
            text_sum[...] = text_terms(jnp.concatenate(parts), 0, total)
            text_send[...] = text_sum[...].astype(jnp.bfloat16)
            for copy in text_scatter:
                copy.start()
    else:
        for copy in image_gather:
            copy.wait_recv()
        text_sum[...] = jnp.zeros_like(text_sum)

        def step(at, carry):
            begin = pl.multiple_of(at * chunk, chunk)
            weights = weights_of(begin)
            terms = image_terms(weights)

            @pl.when(at == 0)
            def _():
                image_own[...] = terms[:rows]

            image_send[pl.ds(begin, chunk)] = terms.astype(jnp.bfloat16)
            text_sum[...] += text_terms(weights, begin, chunk)
            return carry

        lax.fori_loop(0, total // chunk, step, 0)
        for copy in image_scatter:
            copy.start()
        text_send[...] = text_sum[...].astype(jnp.bfloat16)
        for copy in text_scatter:
            copy.start()

    for copy in image_scatter:
        copy.wait_recv()
    grads = image_own[...]
    for s in image_slots:
        grads += image_got[s].astype(jnp.float32)
    outs[0] = grads
    for copy in text_scatter:
        copy.wait_recv()
    grads = text_sum[pl.ds(0, rows)]
    for s in text_slots:
        grads += text_got[s].astype(jnp.float32)
    outs[1] = grads
    for copy in text_gather + image_gather + image_scatter + text_scatter:
        copy.wait_send()


def local(n_blk, n_grp, image_embeds, text_embeds):
    rows, width = image_embeds.shape
    pair = 2 if n_grp % 2 == 0 else 1
    blk_inner = 2 if n_blk % 2 == 0 else 1
    n_image, n_text = n_blk * pair, n_grp // pair
    total = n_image * rows
    chunk = total // SPLIT if total <= 256 else 128
    bf16, f32 = jnp.bfloat16, jnp.float32
    out = jax.ShapeDtypeStruct((rows, width), f32)
    sums = pl.pallas_call(
        functools.partial(kernel, n_blk, n_grp, blk_inner, pair, rows, chunk),
        out_shape=jax.ShapeDtypeStruct((2, rows, width), f32),
        in_specs=[pl.BlockSpec(memory_space=pl.ANY)] * 2,
        out_specs=pl.BlockSpec(memory_space=pltpu.VMEM),
        scratch_shapes=[
            pltpu.VMEM((total, width), bf16),
            pltpu.VMEM((n_text * rows, width), bf16),
            pltpu.VMEM((total, width), bf16),
            pltpu.VMEM((n_text * rows, width), bf16),
            pltpu.VMEM((n_image, rows, width), bf16),
            pltpu.VMEM((n_text, rows, width), bf16),
            pltpu.VMEM((n_text * rows, width), f32),
            pltpu.VMEM((rows, width), f32),
            pltpu.SemaphoreType.DMA((2,)),
            *[pltpu.SemaphoreType.DMA((n,)) for n in (n_image, n_image, n_text, n_text) * 2],
        ],
        compiler_params=pltpu.CompilerParams(
            collective_id=0, has_side_effects=True, vmem_limit_bytes=40 * 1024 * 1024
        ),
    )(image_embeds, text_embeds)
    return sums[0], sums[1]


def solution(mesh):
    placed = (P(("blk", "grp"), None), P(("blk", "grp"), None))
    return jax.shard_map(
        functools.partial(local, mesh.shape["blk"], mesh.shape["grp"]),
        mesh=mesh,
        in_specs=placed,
        out_specs=placed,
        check_vma=False,
    )
```

```python
import functools

import jax
import jax.numpy as jnp
from jax import lax
from jax.experimental import pallas as pl
from jax.experimental.pallas import tpu as pltpu
from jax.sharding import PartitionSpec as P

LOGIT_SCALE = 0.044
LOGIT_BIAS = -4.0
SPLIT = 1
TEXT_FIRST = True
MESH = pl.DeviceIdType.MESH


def offsets(count, inner):
    return [(o, i) for o in range(count // inner) for i in range(inner)]


def moved(index, count, inner, step, sign):
    outer = lax.rem(index // inner + sign * step[0] + count // inner, count // inner)
    return outer * inner + lax.rem(index % inner + sign * step[1] + inner, inner)


def kernel(
    n_blk, n_grp, blk_inner, pair, rows, chunk,
    image_ref, text_ref, outs,
    images, texts, image_send, text_send, image_got, text_got, text_sum, image_own,
    local_sem, gi_send, gi_recv, gt_send, gt_recv, si_send, si_recv, st_send, st_recv,
):
    blk, grp = lax.axis_index("blk"), lax.axis_index("grp")
    image_steps = [(b, c) for b in offsets(n_blk, blk_inner) for c in range(pair)]
    text_steps = list(range(n_grp // pair))

    def image_peer(step, sign):
        return (moved(blk, n_blk, blk_inner, step[0], sign), moved(grp, n_grp, pair, (0, step[1]), sign))

    def text_peer(step, sign):
        return (blk, moved(grp, n_grp, pair, (step, 0), sign))

    image_slots = range(1, len(image_steps))
    text_slots = range(1, len(text_steps))

    own_image = pltpu.make_async_copy(image_ref, images.at[pl.ds(0, rows)], local_sem.at[0])
    own_text = pltpu.make_async_copy(text_ref, texts.at[pl.ds(0, rows)], local_sem.at[1])

    barrier = pltpu.get_barrier_semaphore()
    for s in text_slots[::-1]:
        pl.semaphore_signal(barrier, inc=1, device_id=text_peer(text_steps[s], 1), device_id_type=MESH)
    for s in image_slots[::-1]:
        pl.semaphore_signal(barrier, inc=1, device_id=image_peer(image_steps[s], 1), device_id_type=MESH)
    pl.semaphore_wait(barrier, len(image_slots) + len(text_slots))

    def remote(src, dst, send, recv, slot, device):
        return pltpu.make_async_remote_copy(
            src_ref=src, dst_ref=dst, send_sem=send.at[slot], recv_sem=recv.at[slot],
            device_id=device, device_id_type=MESH,
        )

    def part(ref, slot):
        return ref.at[pl.ds(slot * rows, rows)]

    text_gather = [
        remote(text_ref, part(texts, s), gt_send, gt_recv, s, text_peer(text_steps[s], 1))
        for s in text_slots
    ]
    image_gather = [
        remote(image_ref, part(images, s), gi_send, gi_recv, s, image_peer(image_steps[s], 1))
        for s in image_slots
    ]
    order = image_gather[2::2] + text_gather[::-1] + image_gather[1::2] + image_gather[:1]
    for copy in order:
        copy.start()
    own_text.start()
    own_image.start()
    total = images.shape[0]

    def weights_of(begin):
        logits = LOGIT_SCALE * lax.dot_general(
            images[pl.ds(begin, chunk)], texts[...], (((1,), (1,)), ((), ())),
            preferred_element_type=jnp.float32,
        ) + LOGIT_BIAS
        row = lax.broadcasted_iota(jnp.int32, logits.shape, 0) + begin
        column = lax.broadcasted_iota(jnp.int32, logits.shape, 1)
        labels = jnp.where((row == column) & (row < rows), 1.0, 0.0)
        return (lax.logistic(logits) - labels).astype(jnp.bfloat16)

    def image_terms(weights):
        return LOGIT_SCALE * jnp.dot(weights, texts[...], preferred_element_type=jnp.float32)

    def text_terms(weights, begin, count):
        return LOGIT_SCALE * lax.dot_general(
            weights, images[pl.ds(begin, count)], (((0,), (0,)), ((), ())),
            preferred_element_type=jnp.float32,
        )

    image_scatter = [
        remote(part(image_send, s), image_got.at[s], si_send, si_recv, s, image_peer(image_steps[s], -1))
        for s in image_slots
    ]
    text_scatter = [
        remote(part(text_send, s), text_got.at[s], st_send, st_recv, s, text_peer(text_steps[s], -1))
        for s in text_slots
    ]

    def arrived(begin):
        for copy in image_gather[max(begin // rows - 1, 0):(begin + chunk) // rows - 1]:
            copy.wait_recv()

    own_text.wait()
    own_image.wait()
    for copy in text_gather:
        copy.wait_recv()
    if total <= 256:
        parts = []
        for begin in range(0, total, chunk):
            arrived(begin)
            parts.append(weights_of(begin))
            if TEXT_FIRST and begin + chunk == total:
                text_sum[...] = text_terms(jnp.concatenate(parts), 0, total)
                text_send[...] = text_sum[...].astype(jnp.bfloat16)
                for copy in text_scatter:
                    copy.start()
            terms = image_terms(parts[-1])
            if begin == 0:
                image_own[...] = terms[:rows]
            image_send[pl.ds(begin, chunk)] = terms.astype(jnp.bfloat16)
            sends = image_scatter[max(begin // rows - 1, 0):(begin + chunk) // rows - 1]
            for copy in sends[2::2] + sends[1::2] + sends[:1]:
                copy.start()
        if not TEXT_FIRST:
            text_sum[...] = text_terms(jnp.concatenate(parts), 0, total)
            text_send[...] = text_sum[...].astype(jnp.bfloat16)
            for copy in text_scatter:
                copy.start()
    else:
        for copy in image_gather:
            copy.wait_recv()
        text_sum[...] = jnp.zeros_like(text_sum)

        def step(at, carry):
            begin = pl.multiple_of(at * chunk, chunk)
            weights = weights_of(begin)
            terms = image_terms(weights)

            @pl.when(at == 0)
            def _():
                image_own[...] = terms[:rows]

            image_send[pl.ds(begin, chunk)] = terms.astype(jnp.bfloat16)
            text_sum[...] += text_terms(weights, begin, chunk)
            return carry

        lax.fori_loop(0, total // chunk, step, 0)
        for copy in image_scatter:
            copy.start()
        text_send[...] = text_sum[...].astype(jnp.bfloat16)
        for copy in text_scatter:
            copy.start()

    for copy in text_gather + image_gather + image_scatter + text_scatter:
        copy.wait_send()
    for copy in image_scatter:
        copy.wait_recv()
    grads = image_own[...]
    for s in image_slots:
        grads += image_got[s].astype(jnp.float32)
    outs[0] = grads
    for copy in text_scatter:
        copy.wait_recv()
    grads = text_sum[pl.ds(0, rows)]
    for s in text_slots:
        grads += text_got[s].astype(jnp.float32)
    outs[1] = grads


def local(n_blk, n_grp, image_embeds, text_embeds):
    rows, width = image_embeds.shape
    pair = 2 if n_grp % 2 == 0 else 1
    blk_inner = 2 if n_blk % 2 == 0 else 1
    n_image, n_text = n_blk * pair, n_grp // pair
    total = n_image * rows
    chunk = total // SPLIT if total <= 256 else 128
    bf16, f32 = jnp.bfloat16, jnp.float32
    out = jax.ShapeDtypeStruct((rows, width), f32)
    sums = pl.pallas_call(
        functools.partial(kernel, n_blk, n_grp, blk_inner, pair, rows, chunk),
        out_shape=jax.ShapeDtypeStruct((2, rows, width), f32),
        in_specs=[pl.BlockSpec(memory_space=pl.ANY)] * 2,
        out_specs=pl.BlockSpec(memory_space=pltpu.VMEM),
        scratch_shapes=[
            pltpu.VMEM((total, width), bf16),
            pltpu.VMEM((n_text * rows, width), bf16),
            pltpu.VMEM((total, width), bf16),
            pltpu.VMEM((n_text * rows, width), bf16),
            pltpu.VMEM((n_image, rows, width), bf16),
            pltpu.VMEM((n_text, rows, width), bf16),
            pltpu.VMEM((n_text * rows, width), f32),
            pltpu.VMEM((rows, width), f32),
            pltpu.SemaphoreType.DMA((2,)),
            *[pltpu.SemaphoreType.DMA((n,)) for n in (n_image, n_image, n_text, n_text) * 2],
        ],
        compiler_params=pltpu.CompilerParams(
            collective_id=0, has_side_effects=True, vmem_limit_bytes=40 * 1024 * 1024
        ),
    )(image_embeds, text_embeds)
    return sums[0], sums[1]


def solution(mesh):
    placed = (P(("blk", "grp"), None), P(("blk", "grp"), None))
    return jax.shard_map(
        functools.partial(local, mesh.shape["blk"], mesh.shape["grp"]),
        mesh=mesh,
        in_specs=placed,
        out_specs=placed,
        check_vma=False,
    )
```

```python
import functools

import jax
import jax.numpy as jnp
from jax import lax
from jax.experimental import pallas as pl
from jax.experimental.pallas import tpu as pltpu
from jax.sharding import PartitionSpec as P

LOGIT_SCALE = 0.044
LOGIT_BIAS = -4.0
SPLIT = 1
TEXT_FIRST = True
MESH = pl.DeviceIdType.MESH


def offsets(count, inner):
    return [(o, i) for o in range(count // inner) for i in range(inner)]


def moved(index, count, inner, step, sign):
    outer = lax.rem(index // inner + sign * step[0] + count // inner, count // inner)
    return outer * inner + lax.rem(index % inner + sign * step[1] + inner, inner)


def kernel(
    n_blk, n_grp, blk_inner, pair, rows, chunk,
    image_ref, text_ref, outs,
    images, texts, image_send, text_send, image_got, text_got, text_sum, image_own,
    local_sem, gi_send, gi_recv, gt_send, gt_recv, si_send, si_recv, st_send, st_recv,
):
    blk, grp = lax.axis_index("blk"), lax.axis_index("grp")
    image_steps = [(b, c) for b in offsets(n_blk, blk_inner) for c in range(pair)]
    text_steps = list(range(n_grp // pair))

    def image_peer(step, sign):
        return (moved(blk, n_blk, blk_inner, step[0], sign), moved(grp, n_grp, pair, (0, step[1]), sign))

    def text_peer(step, sign):
        return (blk, moved(grp, n_grp, pair, (step, 0), sign))

    image_slots = range(1, len(image_steps))
    text_slots = range(1, len(text_steps))

    own_image = pltpu.make_async_copy(image_ref, images.at[pl.ds(0, rows)], local_sem.at[0])
    own_text = pltpu.make_async_copy(text_ref, texts.at[pl.ds(0, rows)], local_sem.at[1])

    barrier = pltpu.get_barrier_semaphore()
    for s in text_slots[::-1]:
        pl.semaphore_signal(barrier, inc=1, device_id=text_peer(text_steps[s], 1), device_id_type=MESH)
    for s in image_slots[::-1]:
        pl.semaphore_signal(barrier, inc=1, device_id=image_peer(image_steps[s], 1), device_id_type=MESH)
    pl.semaphore_wait(barrier, len(image_slots) + len(text_slots))

    def remote(src, dst, send, recv, slot, device):
        return pltpu.make_async_remote_copy(
            src_ref=src, dst_ref=dst, send_sem=send.at[slot], recv_sem=recv.at[slot],
            device_id=device, device_id_type=MESH,
        )

    def part(ref, slot):
        return ref.at[pl.ds(slot * rows, rows)]

    text_gather = [
        remote(text_ref, part(texts, s), gt_send, gt_recv, s, text_peer(text_steps[s], 1))
        for s in text_slots
    ]
    image_gather = [
        remote(image_ref, part(images, s), gi_send, gi_recv, s, image_peer(image_steps[s], 1))
        for s in image_slots
    ]
    order = image_gather[2::2] + text_gather[::-1] + image_gather[1::2] + image_gather[:1]
    for copy in order:
        copy.start()
    own_text.start()
    own_image.start()
    total = images.shape[0]

    def weights_of(begin):
        logits = LOGIT_SCALE * lax.dot_general(
            images[pl.ds(begin, chunk)], texts[...], (((1,), (1,)), ((), ())),
            preferred_element_type=jnp.float32,
        ) + LOGIT_BIAS
        row = lax.broadcasted_iota(jnp.int32, logits.shape, 0) + begin
        column = lax.broadcasted_iota(jnp.int32, logits.shape, 1)
        labels = jnp.where((row == column) & (row < rows), 1.0, 0.0)
        return (lax.logistic(logits) - labels).astype(jnp.bfloat16)

    def image_terms(weights):
        return LOGIT_SCALE * jnp.dot(weights, texts[...], preferred_element_type=jnp.float32)

    def text_terms(weights, begin, count):
        return LOGIT_SCALE * lax.dot_general(
            weights, images[pl.ds(begin, count)], (((0,), (0,)), ((), ())),
            preferred_element_type=jnp.float32,
        )

    image_scatter = [
        remote(part(image_send, s), image_got.at[s], si_send, si_recv, s, image_peer(image_steps[s], -1))
        for s in image_slots
    ]
    text_scatter = [
        remote(part(text_send, s), text_got.at[s], st_send, st_recv, s, text_peer(text_steps[s], -1))
        for s in text_slots
    ]

    def arrived(begin):
        for copy in image_gather[max(begin // rows - 1, 0):(begin + chunk) // rows - 1]:
            copy.wait_recv()

    own_text.wait()
    own_image.wait()
    for copy in text_gather:
        copy.wait_recv()
    if total <= 256:
        parts = []
        for begin in range(0, total, chunk):
            arrived(begin)
            parts.append(weights_of(begin))
            if TEXT_FIRST and begin + chunk == total:
                text_sum[...] = text_terms(jnp.concatenate(parts), 0, total)
                text_send[...] = text_sum[...].astype(jnp.bfloat16)
                for copy in text_scatter[::-1]:
                    copy.start()
            terms = image_terms(parts[-1])
            if begin == 0:
                image_own[...] = terms[:rows]
            image_send[pl.ds(begin, chunk)] = terms.astype(jnp.bfloat16)
            sends = image_scatter[max(begin // rows - 1, 0):(begin + chunk) // rows - 1]
            for copy in sends[2::2] + sends[1::2] + sends[:1]:
                copy.start()
        if not TEXT_FIRST:
            text_sum[...] = text_terms(jnp.concatenate(parts), 0, total)
            text_send[...] = text_sum[...].astype(jnp.bfloat16)
            for copy in text_scatter:
                copy.start()
    else:
        for copy in image_gather:
            copy.wait_recv()
        text_sum[...] = jnp.zeros_like(text_sum)

        def step(at, carry):
            begin = pl.multiple_of(at * chunk, chunk)
            weights = weights_of(begin)
            terms = image_terms(weights)

            @pl.when(at == 0)
            def _():
                image_own[...] = terms[:rows]

            image_send[pl.ds(begin, chunk)] = terms.astype(jnp.bfloat16)
            text_sum[...] += text_terms(weights, begin, chunk)
            return carry

        lax.fori_loop(0, total // chunk, step, 0)
        for copy in image_scatter:
            copy.start()
        text_send[...] = text_sum[...].astype(jnp.bfloat16)
        for copy in text_scatter:
            copy.start()

    for copy in text_gather + image_gather + image_scatter + text_scatter:
        copy.wait_send()
    grads = image_own[...]
    for s in image_slots:
        image_scatter[s - 1].wait_recv()
        grads += image_got[s].astype(jnp.float32)
    outs[0] = grads
    grads = text_sum[pl.ds(0, rows)]
    for s in text_slots:
        text_scatter[s - 1].wait_recv()
        grads += text_got[s].astype(jnp.float32)
    outs[1] = grads


def local(n_blk, n_grp, image_embeds, text_embeds):
    rows, width = image_embeds.shape
    pair = 2 if n_grp % 2 == 0 else 1
    blk_inner = 2 if n_blk % 2 == 0 else 1
    n_image, n_text = n_blk * pair, n_grp // pair
    total = n_image * rows
    chunk = total // SPLIT if total <= 256 else 128
    bf16, f32 = jnp.bfloat16, jnp.float32
    out = jax.ShapeDtypeStruct((rows, width), f32)
    sums = pl.pallas_call(
        functools.partial(kernel, n_blk, n_grp, blk_inner, pair, rows, chunk),
        out_shape=jax.ShapeDtypeStruct((2, rows, width), f32),
        in_specs=[pl.BlockSpec(memory_space=pl.ANY)] * 2,
        out_specs=pl.BlockSpec(memory_space=pltpu.VMEM),
        scratch_shapes=[
            pltpu.VMEM((total, width), bf16),
            pltpu.VMEM((n_text * rows, width), bf16),
            pltpu.VMEM((total, width), bf16),
            pltpu.VMEM((n_text * rows, width), bf16),
            pltpu.VMEM((n_image, rows, width), bf16),
            pltpu.VMEM((n_text, rows, width), bf16),
            pltpu.VMEM((n_text * rows, width), f32),
            pltpu.VMEM((rows, width), f32),
            pltpu.SemaphoreType.DMA((2,)),
            *[pltpu.SemaphoreType.DMA((n,)) for n in (n_image, n_image, n_text, n_text) * 2],
        ],
        compiler_params=pltpu.CompilerParams(
            collective_id=0, has_side_effects=True, vmem_limit_bytes=40 * 1024 * 1024
        ),
    )(image_embeds, text_embeds)
    return sums[0], sums[1]


def solution(mesh):
    placed = (P(("blk", "grp"), None), P(("blk", "grp"), None))
    return jax.shard_map(
        functools.partial(local, mesh.shape["blk"], mesh.shape["grp"]),
        mesh=mesh,
        in_specs=placed,
        out_specs=placed,
        check_vma=False,
    )
```
